32 devices in a mesh: group: 2 (over y), stn: 8 (over z, x), chan: 2 (over core).
Axes of the slice: x: 2, y: 2, z: 4, core: 2. Of those that a mesh axis runs over, the one named last changes fastest.
Arguments:
- gradient: float32 [65536], P(('group', 'stn')), parts along dimension 0, may hold values from -24 to 24
- normal_blocks: bfloat16 [2, 512, 5, 128, 128], P('chan', ('group', 'stn')), parts along dimension 1, may hold values from -0.2 to 4.2
- pattern: int32 [512, 5], P(('group', 'stn')), parts along dimension 0, may hold values from 0 to 255, as said below
Outputs:
- solution: float32 [65536], P(('group', 'stn')), parts along dimension 0
- residual: float32 [65536], P(('group', 'stn')), parts along dimension 0
The draws below stay inside these ranges and needn't reach their ends.
There are 2 independent parts, one for each index of `group`. The reference program is written for one: setup_inputs(seed, part) draws one part's arguments, and reference() takes and returns one part's arrays. A program takes and returns all parts, laid end to end along the dimension named above; each array names one. Nothing has to cross between parts.
Inputs may be any that keep to these rules, and one draw needn't show every extreme that they name: pattern[n, 0] = n. Block rows come in station groups of 32 (group n // 32); tile 3 lies in the group exactly 4 away from that of n; every other column block of row n lies in a group whose number differs from that of n by at most 3 modulo 8, tile 1 exactly 3 groups ahead and tile 2 exactly 3 behind.
All inputs are finite; a program needn't handle non-finite values.
Results may differ from the reference program's by a relative error of at most 0.011.
Values may be sent and summed in bfloat16 or wider, within the bound.
A program may use at most 64 MiB of HBM per device.

```python
import math
import jax
import jax.numpy as jnp

BLK = 128
TILES = 5
REACH = 3
ITERS = 2
UNK_DEV = 4096
BLK_DEV = 32
UNK = 32768
NB = 256
N_STN = 8
N_CHAN = 2


def draw_pattern(key, part):
    key = jax.random.fold_in(key, 1)
    key_block, key_offset = jax.random.split(key)
    rows = jnp.arange(NB, dtype=jnp.int32)
    owners = rows // BLK_DEV
    picks = jax.random.randint(key_block, (NB, TILES), 0, BLK_DEV, dtype=jnp.int32)
    offsets = jax.random.randint(key_offset, (NB, TILES), -REACH, REACH + 1, dtype=jnp.int32)
    offsets = offsets.at[:, 1].set(REACH).at[:, 2].set(-REACH).at[:, 3].set(N_STN // 2)
    columns = (owners[:, None] + offsets) % N_STN * BLK_DEV + picks
    columns = columns.at[:, 0].set(rows)
    return columns.astype(jnp.int32)


def draw_normal_blocks(key, part):
    key = jax.random.fold_in(key, 2)
    key_off, key_diag, key_level, key_row = jax.random.split(key, 4)
    shape = (N_CHAN, NB, TILES, BLK, BLK)
    owners = jnp.arange(NB, dtype=jnp.int32) // BLK_DEV
    spread = jnp.clip(jax.random.normal(key_off, shape, jnp.float32), -4.0, 4.0) * 0.035
    diag = jax.random.uniform(key_diag, (N_CHAN, NB, BLK), jnp.float32, 2.0, 4.0)
    level = jnp.exp(jax.random.uniform(key_level, (N_STN,), jnp.float32, math.log(0.1), math.log(0.64)))
    row_factor = jnp.exp(jax.random.uniform(key_row, (N_CHAN, NB), jnp.float32, math.log(0.7), math.log(1.4)))
    mean = level[owners][None, :] * row_factor / BLK
    tile_mask = (jnp.arange(TILES) >= 1).astype(jnp.float32)
    coupling = mean[:, :, None, None, None] * tile_mask[None, None, :, None, None]
    eye = jnp.eye(BLK, dtype=jnp.float32)
    blocks = (spread + coupling).at[:, :, 0].add(diag[:, :, :, None] * eye)
    return blocks.astype(jnp.bfloat16)


def draw_gradient(key, part):
    key = jax.random.fold_in(key, 3)
    key_value, key_factor, key_level = jax.random.split(key, 3)
    place = jnp.arange(UNK, dtype=jnp.float32) / (UNK - 1)
    owners = jnp.arange(UNK, dtype=jnp.int32) // UNK_DEV
    factor = jnp.exp(jax.random.uniform(key_factor, (UNK,), jnp.float32, math.log(0.5), math.log(2.0)))
    value = jnp.clip(jax.random.normal(key_value, (UNK,), jnp.float32), -3.0, 3.0)
    rise = jnp.exp(math.log(3.0) * place)
    level = jnp.exp(jax.random.uniform(key_level, (N_STN,), jnp.float32, math.log(0.4), math.log(4.0)))
    return value * rise * factor + level[owners]


def setup_inputs(seed: int = 0, part: int = 0) -> dict:
    splits = jax.random.split(jax.random.key(seed), 4)
    part_splits = jax.random.split(jax.random.fold_in(splits[3], part), 4)
    gradient = draw_gradient(jax.random.fold_in(jax.random.fold_in(splits[3], part), 71), part)
    normal_blocks = draw_normal_blocks(jax.random.fold_in(jax.random.fold_in(splits[3], part), 71), part)
    pattern = draw_pattern(jax.random.fold_in(jax.random.fold_in(splits[3], part), 71), part)
    return {"gradient": gradient, "normal_blocks": normal_blocks, "pattern": pattern}


def apply_operator(vector, normal_blocks, pattern):
    rounded = vector.astype(jnp.bfloat16).reshape(NB, BLK)
    picked = rounded[pattern].astype(jnp.float32)
    total = jnp.zeros((NB, BLK), jnp.float32)
    for band in range(N_CHAN):
        total = total + jnp.einsum("nkij,nkj->ni", normal_blocks[band].astype(jnp.float32), picked)
    return total.reshape(UNK)


def reference(gradient, normal_blocks, pattern):
    solution = jnp.zeros_like(gradient)
    residual = gradient
    direction = gradient
    norm_now = jnp.sum(residual * residual)
    for step in range(ITERS):
        image = apply_operator(direction, normal_blocks, pattern)
        alpha = norm_now / jnp.sum(direction * image)
        solution = solution + alpha * direction
        residual = residual - alpha * image
        norm_next = jnp.sum(residual * residual)
        direction = residual + (norm_next / norm_now) * direction
        norm_now = norm_next
    return solution, residual
```

```python
import functools

import jax
import jax.numpy as jnp
from jax import lax
from jax.experimental import pallas as pl
from jax.experimental.pallas import tpu as pltpu
from jax.sharding import PartitionSpec as P

MESH = pl.DeviceIdType.MESH
ROWS = 16
REACH = 3


def near_offsets(n):
    near = {n // 2}
    for k in range(1, REACH + 1):
        near |= {k % n, (n - k) % n}
    return sorted(near - {0})


def kernel(
    n, chans, pattern, gradient, blocks_hbm, solution, residual,
    blocks, sent0, sent1, whole, picked, mine, theirs, sums0, sums1,
    load_sem, send_sem, recv_sem,
):
    me = lax.axis_index("stn")
    chan = lax.axis_index("chan")
    slot = me * chans + chan
    block_rows, width = gradient.shape
    tiles = blocks.shape[1]
    near = near_offsets(n)
    peers = [(o, c) for o in range(n) for c in range(chans) if (o, c) != (0, 0)]

    load = pltpu.make_async_copy(blocks_hbm.at[0], blocks, load_sem)
    load.start()

    def at(offset, turn):
        return {"stn": lax.rem(me + offset, n), "chan": lax.rem(chan + turn, chans)}

    barrier = pltpu.get_barrier_semaphore()
    for o, c in peers:
        pl.semaphore_signal(barrier, inc=1, device_id=at(o, c), device_id_type=MESH)

    g = gradient[...]
    sent0[me] = g.astype(jnp.bfloat16)
    sums0[slot] = jnp.zeros((8, width), jnp.float32)
    sums1[slot] = jnp.zeros((8, width), jnp.float32)
    pl.semaphore_wait(barrier, len(peers))

    def send(src, dst, which, offset, turn):
        pltpu.make_async_remote_copy(
            src_ref=src, dst_ref=dst, send_sem=send_sem.at[which],
            recv_sem=recv_sem.at[which], device_id=at(offset, turn), device_id_type=MESH,
        ).start()

    def wait(ref, sem):
        pltpu.make_async_copy(ref, ref, sem).wait()

    def apply(sent):
        for o in [0] + near:
            s = lax.rem(me + o, n)
            whole[pl.ds(pl.multiple_of(s * block_rows, block_rows), block_rows), :] = (
                sent[s].astype(jnp.float32)
            )
        for r in range(block_rows):
            for k in range(tiles):
                picked[r : r + 1, k * width : (k + 1) * width] = whole[
                    pl.ds(pattern[k, r], 1), :
                ]
        row = lax.broadcasted_iota(jnp.int32, (ROWS, width), 0)
        out = []
        for base in range(0, block_rows, ROWS):
            left = picked[base : base + ROWS, :].astype(jnp.bfloat16)
            total = jnp.zeros((ROWS, width), jnp.float32)
            for m in range(0, ROWS, 2):
                right = jnp.concatenate(
                    [
                        jnp.concatenate(
                            [blocks[base + m + j, k] for k in range(tiles)], axis=1
                        )
                        for j in range(2)
                    ],
                    axis=0,
                )
                both = lax.dot_general(
                    left, right, (((1,), (1,)), ((), ())),
                    preferred_element_type=jnp.float32,
                )
                total = jnp.where(row == m, both[:, :width], total)
                total = jnp.where(row == m + 1, both[:, width:], total)
            out.append(total)
        return jnp.concatenate(out, axis=0)

    def rowsum(value):
        return jnp.sum(value, axis=0, keepdims=True)

    def total_of(sums):
        return jnp.sum(jnp.sum(sums[...], axis=0), axis=1, keepdims=True)

    for o in near:
        send(sent0.at[me], sent0.at[me], 0, o, 0)
    load.wait()
    wait(sent0.at[pl.ds(0, len(near))], recv_sem.at[0])
    part0 = apply(sent0)

    mine[0] = part0
    send(mine.at[0], theirs.at[0], 1, 0, 1)
    sums0[slot, 0:1, :] = rowsum(g * g)
    sums0[slot, 1:2, :] = rowsum(g * part0)
    for o, c in peers:
        send(sums0.at[slot], sums0.at[slot], 2, o, c)
    wait(theirs.at[0], recv_sem.at[1])
    image = part0 + theirs[0]
    wait(sums0.at[pl.ds(0, len(peers))], recv_sem.at[2])
    totals = total_of(sums0)
    norm0 = totals[0:1, :] * (1.0 / chans)
    curve0 = totals[1:2, :]
    alpha0 = norm0 / curve0
    r1 = g - alpha0 * image

    sent1[me] = r1.astype(jnp.bfloat16)
    for o in near:
        send(sent1.at[me], sent1.at[me], 3, o, 0)
    wait(sent1.at[pl.ds(0, len(near))], recv_sem.at[3])
    part1 = apply(sent1)

    mine[1] = part1
    send(mine.at[1], theirs.at[1], 4, 0, 1)
    sums1[slot, 0:1, :] = rowsum(r1 * r1)
    sums1[slot, 1:2, :] = rowsum(r1 * part1)
    sums1[slot, 2:3, :] = rowsum(r1 * part0 + g * part1)
    for o, c in peers:
        send(sums1.at[slot], sums1.at[slot], 5, o, c)
    wait(theirs.at[1], recv_sem.at[4])
    image1 = part1 + theirs[1]
    wait(sums1.at[pl.ds(0, len(peers))], recv_sem.at[5])
    totals = total_of(sums1)
    norm1 = totals[0:1, :] * (1.0 / chans)
    beta = norm1 / norm0
    curve1 = totals[1:2, :] + beta * (totals[2:3, :] + beta * curve0)
    alpha1 = norm1 / curve1
    solution[...] = alpha0 * g + alpha1 * (r1 + beta * g)
    residual[...] = r1 - alpha1 * (image1 + beta * image)

    wait(sent0.at[pl.ds(0, len(near))], send_sem.at[0])
    wait(theirs.at[0], send_sem.at[1])
    wait(sums0.at[pl.ds(0, len(peers))], send_sem.at[2])
    wait(sent1.at[pl.ds(0, len(near))], send_sem.at[3])
    wait(theirs.at[1], send_sem.at[4])
    wait(sums1.at[pl.ds(0, len(peers))], send_sem.at[5])


def solution(mesh):
    n = mesh.shape["stn"]
    chans = mesh.shape["chan"]

    def local(gradient, normal_blocks, pattern):
        _, block_rows, tiles, width, _ = normal_blocks.shape
        f32, bf16 = jnp.float32, jnp.bfloat16
        vector = jax.ShapeDtypeStruct((block_rows, width), f32)
        vmem = pl.BlockSpec(memory_space=pltpu.VMEM)
        sol, res = pl.pallas_call(
            functools.partial(kernel, n, chans),
            out_shape=(vector, vector),
            in_specs=[
                pl.BlockSpec(memory_space=pltpu.SMEM),
                vmem,
                pl.BlockSpec(memory_space=pl.ANY),
            ],
            out_specs=(vmem, vmem),
            scratch_shapes=[
                pltpu.VMEM((block_rows, tiles, width, width), bf16),
                pltpu.VMEM((n, block_rows, width), bf16),
                pltpu.VMEM((n, block_rows, width), bf16),
                pltpu.VMEM((n * block_rows, width), f32),
                pltpu.VMEM((block_rows, tiles * width), f32),
                pltpu.VMEM((2, block_rows, width), f32),
                pltpu.VMEM((2, block_rows, width), f32),
                pltpu.VMEM((n * chans, 8, width), f32),
                pltpu.VMEM((n * chans, 8, width), f32),
                pltpu.SemaphoreType.DMA,
                pltpu.SemaphoreType.DMA((6,)),
                pltpu.SemaphoreType.DMA((6,)),
            ],
            compiler_params=pltpu.CompilerParams(
                collective_id=0,
                has_side_effects=True,
                vmem_limit_bytes=60 * 1024 * 1024,
            ),
        )(pattern.T, gradient.reshape(block_rows, width), normal_blocks)
        return sol.reshape(-1), res.reshape(-1)

    placed = (
        P(("group", "stn")),
        P("chan", ("group", "stn"), None, None, None),
        P(("group", "stn"), None),
    )
    return jax.shard_map(
        local,
        mesh=mesh,
        in_specs=placed,
        out_specs=(P(("group", "stn")), P(("group", "stn"))),
        check_vma=False,
    )
```

```python
import functools

import jax
import jax.numpy as jnp
from jax import lax
from jax.experimental import pallas as pl
from jax.experimental.pallas import tpu as pltpu
from jax.sharding import PartitionSpec as P

MESH = pl.DeviceIdType.MESH
ROWS = 16
REACH = 3


def near_offsets(n):
    near = {n // 2}
    for k in range(1, REACH + 1):
        near |= {k % n, (n - k) % n}
    return sorted(near - {0})


def kernel(
    n, chans, pattern, gradient, blocks_hbm, solution, residual,
    blocks, high, low, images, whole, picked, mine, theirs, sums,
    load_sem, send_sem, recv_sem,
):
    me = lax.axis_index("stn")
    chan = lax.axis_index("chan")
    slot = me * chans + chan
    block_rows, width = gradient.shape
    tiles = blocks.shape[1]
    near = near_offsets(n)
    far = [o for o in range(1, n) if o not in near]
    peers = [(o, c) for o in range(n) for c in range(chans) if (o, c) != (0, 0)]

    load = pltpu.make_async_copy(blocks_hbm.at[0], blocks, load_sem)
    load.start()

    def at(offset, turn):
        return {"stn": lax.rem(me + offset, n), "chan": lax.rem(chan + turn, chans)}

    greeted = [(o, 0) for o in range(1, n)] + [(0, c) for c in range(1, chans)]
    barrier = pltpu.get_barrier_semaphore()
    for o, c in greeted:
        pl.semaphore_signal(barrier, inc=1, device_id=at(o, c), device_id_type=MESH)

    g = gradient[...]
    rounded = g.astype(jnp.bfloat16)
    high[me] = rounded
    low[me] = (g - rounded.astype(jnp.float32)).astype(jnp.bfloat16)
    images[me, block_rows:, :] = jnp.zeros((8, width), jnp.float32)
    sums[slot] = jnp.zeros((8, width), jnp.float32)
    pl.semaphore_wait(barrier, len(greeted))

    def send(src, dst, which, offset, turn):
        pltpu.make_async_remote_copy(
            src_ref=src, dst_ref=dst, send_sem=send_sem.at[which],
            recv_sem=recv_sem.at[which], device_id=at(offset, turn), device_id_type=MESH,
        ).start()

    def wait(ref, sem):
        pltpu.make_async_copy(ref, ref, sem).wait()

    def apply(vector_of):
        for o in [0] + near:
            s = lax.rem(me + o, n)
            whole[pl.ds(pl.multiple_of(s * block_rows, block_rows), block_rows), :] = (
                vector_of(s)
            )
        for r in range(block_rows):
            for k in range(tiles):
                picked[r : r + 1, k * width : (k + 1) * width] = whole[
                    pl.ds(pattern[k, r], 1), :
                ]
        row = lax.broadcasted_iota(jnp.int32, (ROWS, width), 0)
        out = []
        for base in range(0, block_rows, ROWS):
            left = picked[base : base + ROWS, :].astype(jnp.bfloat16)
            total = jnp.zeros((ROWS, width), jnp.float32)
            for m in range(0, ROWS, 2):
                right = jnp.concatenate(
                    [
                        jnp.concatenate(
                            [blocks[base + m + j, k] for k in range(tiles)], axis=1
                        )
                        for j in range(2)
                    ],
                    axis=0,
                )
                both = lax.dot_general(
                    left, right, (((1,), (1,)), ((), ())),
                    preferred_element_type=jnp.float32,
                )
                total = jnp.where(row == m, both[:, :width], total)
                total = jnp.where(row == m + 1, both[:, width:], total)
            out.append(total)
        return jnp.concatenate(out, axis=0)

    def rowsum(value):
        return jnp.sum(value, axis=0, keepdims=True)

    def total_of(rows):
        return jnp.sum(jnp.sum(rows, axis=0), axis=1, keepdims=True)

    for o in reversed(near):
        send(high.at[me], high.at[me], 0, o, 0)
    for o in reversed(near):
        send(low.at[me], low.at[me], 1, o, 0)
    load.wait()
    wait(high.at[pl.ds(0, len(near))], recv_sem.at[0])
    part0 = apply(lambda s: high[s].astype(jnp.float32))

    mine[0] = part0
    send(mine.at[0], theirs.at[0], 2, 0, 1)
    images[me, block_rows : block_rows + 1, :] = rowsum(g * g)
    wait(theirs.at[0], recv_sem.at[2])
    image = part0 + theirs[0]

    images[me, :block_rows, :] = image
    images[me, block_rows + 1 : block_rows + 2, :] = rowsum(g * image)
    tail = pl.ds(block_rows, 8)
    for o in reversed(near):
        send(images.at[me], images.at[me], 3, o, 0)
    for o in far:
        send(images.at[me, tail], images.at[me, tail], 4, o, 0)
    wait(low.at[pl.ds(0, len(near))], recv_sem.at[1])
    wait(images.at[pl.ds(0, len(near))], recv_sem.at[3])
    if far:
        wait(images.at[pl.ds(0, len(far)), tail], recv_sem.at[4])
    totals = total_of(images[:, block_rows:, :])
    norm0 = totals[0:1, :]
    curve0 = totals[1:2, :]
    alpha0 = norm0 / curve0
    r1 = g - alpha0 * image
    part1 = apply(
        lambda s: high[s].astype(jnp.float32)
        + (low[s].astype(jnp.float32) - alpha0 * images[s, :block_rows, :])
    )

    sums[slot, 0:1, :] = rowsum(r1 * r1)
    sums[slot, 1:2, :] = rowsum(r1 * part1)
    sums[slot, 2:3, :] = rowsum(r1 * part0 + g * part1)
    for o, c in reversed(peers):
        send(sums.at[slot], sums.at[slot], 5, o, c)
    mine[1] = part1
    send(mine.at[1], theirs.at[1], 6, 0, 1)
    wait(theirs.at[1], recv_sem.at[6])
    image1 = part1 + theirs[1]
    wait(sums.at[pl.ds(0, len(peers))], recv_sem.at[5])
    totals = total_of(sums[...])
    norm1 = totals[0:1, :] * (1.0 / chans)
    beta = norm1 / norm0
    curve1 = totals[1:2, :] + beta * (totals[2:3, :] + beta * curve0)
    alpha1 = norm1 / curve1
    solution[...] = alpha0 * g + alpha1 * (r1 + beta * g)
    residual[...] = r1 - alpha1 * (image1 + beta * image)

    wait(high.at[pl.ds(0, len(near))], send_sem.at[0])
    wait(low.at[pl.ds(0, len(near))], send_sem.at[1])
    wait(theirs.at[0], send_sem.at[2])
    wait(images.at[pl.ds(0, len(near))], send_sem.at[3])
    if far:
        wait(images.at[pl.ds(0, len(far)), tail], send_sem.at[4])
    wait(sums.at[pl.ds(0, len(peers))], send_sem.at[5])
    wait(theirs.at[1], send_sem.at[6])


def solution(mesh):
    n = mesh.shape["stn"]
    chans = mesh.shape["chan"]

    def local(gradient, normal_blocks, pattern):
        _, block_rows, tiles, width, _ = normal_blocks.shape
        f32, bf16 = jnp.float32, jnp.bfloat16
        vector = jax.ShapeDtypeStruct((block_rows, width), f32)
        vmem = pl.BlockSpec(memory_space=pltpu.VMEM)
        sol, res = pl.pallas_call(
            functools.partial(kernel, n, chans),
            out_shape=(vector, vector),
            in_specs=[
                pl.BlockSpec(memory_space=pltpu.SMEM),
                vmem,
                pl.BlockSpec(memory_space=pl.ANY),
            ],
            out_specs=(vmem, vmem),
            scratch_shapes=[
                pltpu.VMEM((block_rows, tiles, width, width), bf16),
                pltpu.VMEM((n, block_rows, width), bf16),
                pltpu.VMEM((n, block_rows, width), bf16),
                pltpu.VMEM((n, block_rows + 8, width), f32),
                pltpu.VMEM((n * block_rows, width), f32),
                pltpu.VMEM((block_rows, tiles * width), f32),
                pltpu.VMEM((2, block_rows, width), f32),
                pltpu.VMEM((2, block_rows, width), f32),
                pltpu.VMEM((n * chans, 8, width), f32),
                pltpu.SemaphoreType.DMA,
                pltpu.SemaphoreType.DMA((7,)),
                pltpu.SemaphoreType.DMA((7,)),
            ],
            compiler_params=pltpu.CompilerParams(
                collective_id=0,
                has_side_effects=True,
                vmem_limit_bytes=60 * 1024 * 1024,
            ),
        )(pattern.T, gradient.reshape(block_rows, width), normal_blocks)
        return sol.reshape(-1), res.reshape(-1)

    placed = (
        P(("group", "stn")),
        P("chan", ("group", "stn"), None, None, None),
        P(("group", "stn"), None),
    )
    return jax.shard_map(
        local,
        mesh=mesh,
        in_specs=placed,
        out_specs=(P(("group", "stn")), P(("group", "stn"))),
        check_vma=False,
    )
```

```python
import functools

import jax
import jax.numpy as jnp
from jax import lax
from jax.experimental import pallas as pl
from jax.experimental.pallas import tpu as pltpu
from jax.sharding import PartitionSpec as P

MESH = pl.DeviceIdType.MESH
ROWS = 16
REACH = 3


def near_offsets(n):
    near = {n // 2}
    for k in range(1, REACH + 1):
        near |= {k % n, (n - k) % n}
    return sorted(near - {0})


def kernel(
    n, chans, pattern_hbm, gradient_hbm, blocks_hbm,
    start_out, step_out, direction_out, before_out, image_out,
       pattern, gradient, blocks, high, low, images, whole, picked, mine, theirs, sums,
    load_sem, send_sem, recv_sem,
):
    me = lax.axis_index("stn")
    chan = lax.axis_index("chan")
    slot = me * chans + chan
    block_rows, width = gradient.shape
    tiles = blocks.shape[1]
    near = near_offsets(n)
    far = [o for o in range(1, n) if o not in near]
    peers = [(o, c) for o in range(n) for c in range(chans) if (o, c) != (0, 0)]

    def at(offset, turn):
        return {"stn": lax.rem(me + offset, n), "chan": lax.rem(chan + turn, chans)}

    greeted = [(o, 0) for o in range(1, n)] + [(0, c) for c in range(1, chans)]
    barrier = pltpu.get_barrier_semaphore()
    for o, c in greeted:
        pl.semaphore_signal(barrier, inc=1, device_id=at(o, c), device_id_type=MESH)

    begin = pltpu.make_async_copy(gradient_hbm, gradient, load_sem.at[0])
    begin.start()
    fetch = pltpu.make_async_copy(pattern_hbm, pattern, load_sem.at[1])
    fetch.start()
    load = pltpu.make_async_copy(blocks_hbm.at[0], blocks, load_sem.at[2])
    load.start()
    begin.wait()
    g = gradient[...]
    rounded = g.astype(jnp.bfloat16)
    high[me] = rounded
    low[me] = (g - rounded.astype(jnp.float32)).astype(jnp.bfloat16)
    images[me, block_rows:, :] = jnp.zeros((8, width), jnp.float32)
    sums[slot] = jnp.zeros((8, width), jnp.float32)
    pl.semaphore_wait(barrier, len(greeted))

    def send(src, dst, which, offset, turn):
        pltpu.make_async_remote_copy(
            src_ref=src, dst_ref=dst, send_sem=send_sem.at[which],
            recv_sem=recv_sem.at[which], device_id=at(offset, turn), device_id_type=MESH,
        ).start()

    def wait(ref, sem):
        pltpu.make_async_copy(ref, ref, sem).wait()

    def apply(vector_of):
        for o in [0] + near:
            s = lax.rem(me + o, n)
            whole[pl.ds(pl.multiple_of(s * block_rows, block_rows), block_rows), :] = (
                vector_of(s)
            )
        for r in range(block_rows):
            for k in range(tiles):
                picked[r : r + 1, k * width : (k + 1) * width] = whole[
                    pl.ds(pattern[k, r], 1), :
                ]
        row = lax.broadcasted_iota(jnp.int32, (ROWS, width), 0)
        out = []
        for base in range(0, block_rows, ROWS):
            left = picked[base : base + ROWS, :].astype(jnp.bfloat16)
            total = jnp.zeros((ROWS, width), jnp.float32)
            for m in range(0, ROWS, 2):
                right = jnp.concatenate(
                    [
                        jnp.concatenate(
                            [blocks[base + m + j, k] for k in range(tiles)], axis=1
                        )
                        for j in range(2)
                    ],
                    axis=0,
                )
                both = lax.dot_general(
                    left, right, (((1,), (1,)), ((), ())),
                    preferred_element_type=jnp.float32,
                )
                total = jnp.where(row == m, both[:, :width], total)
                total = jnp.where(row == m + 1, both[:, width:], total)
            out.append(total)
        return jnp.concatenate(out, axis=0)

    def rowsum(value):
        return jnp.sum(value, axis=0, keepdims=True)

    def total_of(rows):
        return jnp.sum(jnp.sum(rows, axis=0), axis=1, keepdims=True)

    for o in reversed(near):
        send(high.at[me], high.at[me], 0, o, 0)
    for o in reversed(near):
        send(low.at[me], low.at[me], 1, o, 0)
    fetch.wait()
    load.wait()
    wait(high.at[pl.ds(0, len(near))], recv_sem.at[0])
    part0 = apply(lambda s: high[s].astype(jnp.float32))

    mine[0] = part0
    send(mine.at[0], theirs.at[0], 2, 0, 1)
    images[me, block_rows : block_rows + 1, :] = rowsum(g * g)
    wait(theirs.at[0], recv_sem.at[2])
    image = part0 + theirs[0]

    images[me, :block_rows, :] = image
    images[me, block_rows + 1 : block_rows + 2, :] = rowsum(g * image)
    tail = pl.ds(block_rows, 8)
    for o in reversed(near):
        send(images.at[me], images.at[me], 3, o, 0)
    for o in far:
        send(images.at[me, tail], images.at[me, tail], 4, o, 0)
    wait(low.at[pl.ds(0, len(near))], recv_sem.at[1])
    wait(images.at[pl.ds(0, len(near))], recv_sem.at[3])
    if far:
        wait(images.at[pl.ds(0, len(far)), tail], recv_sem.at[4])
    totals = total_of(images[:, block_rows:, :])
    norm0 = totals[0:1, :]
    curve0 = totals[1:2, :]
    alpha0 = norm0 / curve0
    r1 = g - alpha0 * image
    part1 = apply(
        lambda s: high[s].astype(jnp.float32)
        + (low[s].astype(jnp.float32) - alpha0 * images[s, :block_rows, :])
    )

    sums[slot, 0:1, :] = rowsum(r1 * r1)
    sums[slot, 1:2, :] = rowsum(r1 * part1)
    sums[slot, 2:3, :] = rowsum(r1 * part0 + g * part1)
    for o, c in reversed(peers):
        send(sums.at[slot], sums.at[slot], 5, o, c)
    mine[1] = part1
    send(mine.at[1], theirs.at[1], 6, 0, 1)
    wait(theirs.at[1], recv_sem.at[6])
    image1 = part1 + theirs[1]
    wait(sums.at[pl.ds(0, len(peers))], recv_sem.at[5])
    totals = total_of(sums[...])
    norm1 = totals[0:1, :] * (1.0 / chans)
    beta = norm1 / norm0
    curve1 = totals[1:2, :] + beta * (totals[2:3, :] + beta * curve0)
    alpha1 = norm1 / curve1
    step_out[...] = jnp.broadcast_to(alpha1, (block_rows, width))
    start_out[...] = alpha0 * g
    direction_out[...] = r1 + beta * g
    before_out[...] = r1
    image_out[...] = image1 + beta * image

    wait(high.at[pl.ds(0, len(near))], send_sem.at[0])
    wait(low.at[pl.ds(0, len(near))], send_sem.at[1])
    wait(theirs.at[0], send_sem.at[2])
    wait(images.at[pl.ds(0, len(near))], send_sem.at[3])
    if far:
        wait(images.at[pl.ds(0, len(far)), tail], send_sem.at[4])
    wait(sums.at[pl.ds(0, len(peers))], send_sem.at[5])
    wait(theirs.at[1], send_sem.at[6])


def solution(mesh):
    n = mesh.shape["stn"]
    chans = mesh.shape["chan"]

    def local(gradient, normal_blocks, pattern):
        _, block_rows, tiles, width, _ = normal_blocks.shape
        f32, bf16 = jnp.float32, jnp.bfloat16
        vector = jax.ShapeDtypeStruct((block_rows, width), f32)
        vmem = pl.BlockSpec(memory_space=pltpu.VMEM)
        start, alpha, direction, before, image = pl.pallas_call(
            functools.partial(kernel, n, chans),
            out_shape=(vector,) * 5,
            in_specs=[pl.BlockSpec(memory_space=pl.ANY)] * 3,
            out_specs=(vmem,) * 5,
            scratch_shapes=[
                pltpu.SMEM((tiles, block_rows), jnp.int32),
                pltpu.VMEM((block_rows, width), f32),
                pltpu.VMEM((block_rows, tiles, width, width), bf16),
                pltpu.VMEM((n, block_rows, width), bf16),
                pltpu.VMEM((n, block_rows, width), bf16),
                pltpu.VMEM((n, block_rows + 8, width), f32),
                pltpu.VMEM((n * block_rows, width), f32),
                pltpu.VMEM((block_rows, tiles * width), f32),
                pltpu.VMEM((2, block_rows, width), f32),
                pltpu.VMEM((2, block_rows, width), f32),
                pltpu.VMEM((n * chans, 8, width), f32),
                pltpu.SemaphoreType.DMA((3,)),
                pltpu.SemaphoreType.DMA((7,)),
                pltpu.SemaphoreType.DMA((7,)),
            ],
            compiler_params=pltpu.CompilerParams(
                collective_id=0,
                has_side_effects=True,
                vmem_limit_bytes=60 * 1024 * 1024,
            ),
        )(pattern.T, gradient.reshape(block_rows, width), normal_blocks)
        solution = start + alpha * direction
        residual = before - alpha * image
        return solution.reshape(-1), residual.reshape(-1)

    placed = (
        P(("group", "stn")),
        P("chan", ("group", "stn"), None, None, None),
        P(("group", "stn"), None),
    )
    return jax.shard_map(
        local,
        mesh=mesh,
        in_specs=placed,
        out_specs=(P(("group", "stn")), P(("group", "stn"))),
        check_vma=False,
    )
```

```python
import functools

import jax
import jax.numpy as jnp
from jax import lax
from jax.experimental import pallas as pl
from jax.experimental.pallas import tpu as pltpu
from jax.sharding import PartitionSpec as P

MESH = pl.DeviceIdType.MESH
ROWS = 16
REACH = 3


def near_offsets(n):
    near = {n // 2}
    for k in range(1, REACH + 1):
        near |= {k % n, (n - k) % n}
    return sorted(near - {0})


def kernel(
    n, chans, pattern_hbm, gradient_hbm, blocks_hbm,
    start_out, step_out, direction_out, before_out, image_out,
       pattern, gradient, blocks, high, low, images, whole, picked, mine, theirs, sums,
    load_sem, send_sem, recv_sem,
):
    me = lax.axis_index("stn")
    chan = lax.axis_index("chan")
    slot = me * chans + chan
    block_rows, width = gradient.shape
    tiles = blocks.shape[1]
    near = near_offsets(n)
    half = n // 2
    others = [o for o in near if o != half]
    early = [0, 3]
    late = [k for k in range(tiles) if k not in early]
    far = [o for o in range(1, n) if o not in near]
    peers = [(o, c) for o in range(n) for c in range(chans) if (o, c) != (0, 0)]

    def at(offset, turn):
        return {"stn": lax.rem(me + offset, n), "chan": lax.rem(chan + turn, chans)}

    greeted = [(o, 0) for o in range(1, n)] + [(0, c) for c in range(1, chans)]
    barrier = pltpu.get_barrier_semaphore()
    for o, c in greeted:
        pl.semaphore_signal(barrier, inc=1, device_id=at(o, c), device_id_type=MESH)

    begin = pltpu.make_async_copy(gradient_hbm, gradient, load_sem.at[0])
    begin.start()
    fetch = pltpu.make_async_copy(pattern_hbm, pattern, load_sem.at[1])
    fetch.start()
    load = pltpu.make_async_copy(blocks_hbm.at[0], blocks, load_sem.at[2])
    load.start()
    begin.wait()
    g = gradient[...]
    rounded = g.astype(jnp.bfloat16)
    high[me] = rounded
    low[me] = (g - rounded.astype(jnp.float32)).astype(jnp.bfloat16)
    images[me, block_rows:, :] = jnp.zeros((8, width), jnp.float32)
    sums[slot] = jnp.zeros((8, width), jnp.float32)
    pl.semaphore_wait(barrier, len(greeted))

    def send(src, dst, which, offset, turn):
        pltpu.make_async_remote_copy(
            src_ref=src, dst_ref=dst, send_sem=send_sem.at[which],
            recv_sem=recv_sem.at[which], device_id=at(offset, turn), device_id_type=MESH,
        ).start()

    def wait(ref, sem):
        pltpu.make_async_copy(ref, ref, sem).wait()

    def gather(vector_of, offsets, group):
        for o in offsets:
            s = lax.rem(me + o, n)
            whole[pl.ds(pl.multiple_of(s * block_rows, block_rows), block_rows), :] = (
                vector_of(s)
            )
        for r in range(block_rows):
            for k in group:
                picked[r : r + 1, k * width : (k + 1) * width] = whole[
                    pl.ds(pattern[k, r], 1), :
                ]

    def multiply(group):
        row = lax.broadcasted_iota(jnp.int32, (ROWS, width), 0)
        out = []
        for base in range(0, block_rows, ROWS):
            left = jnp.concatenate(
                [
                    picked[base : base + ROWS, k * width : (k + 1) * width]
                    for k in group
                ],
                axis=1,
            ).astype(jnp.bfloat16)
            total = jnp.zeros((ROWS, width), jnp.float32)
            for m in range(0, ROWS, 2):
                right = jnp.concatenate(
                    [
                        jnp.concatenate([blocks[base + m + j, k] for k in group], axis=1)
                        for j in range(2)
                    ],
                    axis=0,
                )
                both = lax.dot_general(
                    left, right, (((1,), (1,)), ((), ())),
                    preferred_element_type=jnp.float32,
                )
                total = jnp.where(row == m, both[:, :width], total)
                total = jnp.where(row == m + 1, both[:, width:], total)
            out.append(total)
        return jnp.concatenate(out, axis=0)

    def rowsum(value):
        return jnp.sum(value, axis=0, keepdims=True)

    def total_of(rows):
        return jnp.sum(jnp.sum(rows, axis=0), axis=1, keepdims=True)

    def first(s):
        return high[s].astype(jnp.float32)

    for o in others[::-1]:
        send(high.at[me], high.at[me], 0, o, 0)
    send(high.at[me], high.at[me], 7, half, 0)
    for o in reversed(near):
        send(low.at[me], low.at[me], 1, o, 0)
    fetch.wait()
    load.wait()
    wait(high.at[0], recv_sem.at[7])
    gather(first, [0, half], early)
    part0 = multiply(early)
    wait(high.at[pl.ds(0, len(others))], recv_sem.at[0])
    gather(first, others, late)
    part0 = part0 + multiply(late)

    mine[0] = part0
    send(mine.at[0], theirs.at[0], 2, 0, 1)
    images[me, block_rows : block_rows + 1, :] = rowsum(g * g)
    wait(theirs.at[0], recv_sem.at[2])
    image = part0 + theirs[0]

    images[me, :block_rows, :] = image
    images[me, block_rows + 1 : block_rows + 2, :] = rowsum(g * image)
    tail = pl.ds(block_rows, 8)
    for o in reversed(near):
        send(images.at[me], images.at[me], 3, o, 0)
    for o in far:
        send(images.at[me, tail], images.at[me, tail], 4, o, 0)
    wait(low.at[pl.ds(0, len(near))], recv_sem.at[1])
    wait(images.at[pl.ds(0, len(near))], recv_sem.at[3])
    if far:
        wait(images.at[pl.ds(0, len(far)), tail], recv_sem.at[4])
    totals = total_of(images[:, block_rows:, :])
    norm0 = totals[0:1, :]
    curve0 = totals[1:2, :]
    alpha0 = norm0 / curve0
    r1 = g - alpha0 * image
    gather(
        lambda s: high[s].astype(jnp.float32)
        + (low[s].astype(jnp.float32) - alpha0 * images[s, :block_rows, :]),
        [0] + near,
        range(tiles),
    )
    part1 = multiply(range(tiles))

    sums[slot, 0:1, :] = rowsum(r1 * r1)
    sums[slot, 1:2, :] = rowsum(r1 * part1)
    sums[slot, 2:3, :] = rowsum(r1 * part0 + g * part1)
    for o, c in reversed(peers):
        send(sums.at[slot, pl.ds(0, 4)], sums.at[slot, pl.ds(0, 4)], 5, o, c)
    mine[1] = part1
    send(mine.at[1], theirs.at[1], 6, 0, 1)
    wait(theirs.at[1], recv_sem.at[6])
    image1 = part1 + theirs[1]
    wait(sums.at[pl.ds(0, len(peers)), pl.ds(0, 4)], recv_sem.at[5])
    totals = total_of(sums[...])
    norm1 = totals[0:1, :] * (1.0 / chans)
    beta = norm1 / norm0
    curve1 = totals[1:2, :] + beta * (totals[2:3, :] + beta * curve0)
    alpha1 = norm1 / curve1
    step_out[...] = jnp.broadcast_to(alpha1, (block_rows, width))
    start_out[...] = alpha0 * g
    direction_out[...] = r1 + beta * g
    before_out[...] = r1
    image_out[...] = image1 + beta * image

    wait(high.at[pl.ds(0, len(others))], send_sem.at[0])
    wait(high.at[0], send_sem.at[7])
    wait(low.at[pl.ds(0, len(near))], send_sem.at[1])
    wait(theirs.at[0], send_sem.at[2])
    wait(images.at[pl.ds(0, len(near))], send_sem.at[3])
    if far:
        wait(images.at[pl.ds(0, len(far)), tail], send_sem.at[4])
    wait(sums.at[pl.ds(0, len(peers)), pl.ds(0, 4)], send_sem.at[5])
    wait(theirs.at[1], send_sem.at[6])


def solution(mesh):
    n = mesh.shape["stn"]
    chans = mesh.shape["chan"]

    def local(gradient, normal_blocks, pattern):
        _, block_rows, tiles, width, _ = normal_blocks.shape
        f32, bf16 = jnp.float32, jnp.bfloat16
        vector = pltpu.VMEM((block_rows, width), f32)
        vmem = pl.BlockSpec(memory_space=pltpu.VMEM)
        start, alpha, direction, before, image = pl.pallas_call(
            functools.partial(kernel, n, chans),
            out_shape=(vector,) * 5,
            in_specs=[pl.BlockSpec(memory_space=pl.ANY)] * 3,
            out_specs=(vmem,) * 5,
            scratch_shapes=[
                pltpu.SMEM((tiles, block_rows), jnp.int32),
                pltpu.VMEM((block_rows, width), f32),
                pltpu.VMEM((block_rows, tiles, width, width), bf16),
                pltpu.VMEM((n, block_rows, width), bf16),
                pltpu.VMEM((n, block_rows, width), bf16),
                pltpu.VMEM((n, block_rows + 8, width), f32),
                pltpu.VMEM((n * block_rows, width), f32),
                pltpu.VMEM((block_rows, tiles * width), f32),
                pltpu.VMEM((2, block_rows, width), f32),
                pltpu.VMEM((2, block_rows, width), f32),
                pltpu.VMEM((n * chans, 8, width), f32),
                pltpu.SemaphoreType.DMA((3,)),
                pltpu.SemaphoreType.DMA((8,)),
                pltpu.SemaphoreType.DMA((8,)),
            ],
            compiler_params=pltpu.CompilerParams(
                collective_id=0,
                has_side_effects=True,
                vmem_limit_bytes=60 * 1024 * 1024,
            ),
        )(pattern.T, gradient.reshape(block_rows, width), normal_blocks)
        solution = start + alpha * direction
        residual = before - alpha * image
        return solution.reshape(-1), residual.reshape(-1)

    placed = (
        P(("group", "stn")),
        P("chan", ("group", "stn"), None, None, None),
        P(("group", "stn"), None),
    )
    return jax.shard_map(
        local,
        mesh=mesh,
        in_specs=placed,
        out_specs=(P(("group", "stn")), P(("group", "stn"))),
        check_vma=False,
    )
```

```python
import functools

import jax
import jax.numpy as jnp
from jax import lax
from jax.experimental import pallas as pl
from jax.experimental.pallas import tpu as pltpu
from jax.sharding import PartitionSpec as P

MESH = pl.DeviceIdType.MESH
ROWS = 16
REACH = 3


def near_offsets(n):
    near = {n // 2}
    for k in range(1, REACH + 1):
        near |= {k % n, (n - k) % n}
    return sorted(near - {0})


def kernel(
    n, chans, pattern_hbm, gradient_hbm, blocks_hbm,
    start_out, step_out, direction_out, before_out, image_out,
       pattern, gradient, blocks, high, low, images, whole, picked, mine, theirs, sums,
    load_sem, send_sem, recv_sem,
):
    me = lax.axis_index("stn")
    chan = lax.axis_index("chan")
    slot = me * chans + chan
    block_rows, width = gradient.shape
    tiles = blocks.shape[1]
    near = near_offsets(n)
    half = n // 2
    others = [o for o in near if o != half]
    early = [0, 3]
    late = [k for k in range(tiles) if k not in early]
    far = [o for o in range(1, n) if o not in near]
    peers = [(o, c) for o in range(n) for c in range(chans) if (o, c) != (0, 0)]

    def at(offset, turn):
        return {"stn": lax.rem(me + offset, n), "chan": lax.rem(chan + turn, chans)}

    greeted = [(o, 0) for o in range(1, n)] + [(0, c) for c in range(1, chans)]
    barrier = pltpu.get_barrier_semaphore()
    for o, c in greeted:
        pl.semaphore_signal(barrier, inc=1, device_id=at(o, c), device_id_type=MESH)

    begin = pltpu.make_async_copy(gradient_hbm, gradient, load_sem.at[0])
    begin.start()
    fetch = pltpu.make_async_copy(pattern_hbm, pattern, load_sem.at[1])
    fetch.start()
    load = pltpu.make_async_copy(blocks_hbm.at[0], blocks, load_sem.at[2])
    load.start()
    begin.wait()
    g = gradient[...]
    rounded = g.astype(jnp.bfloat16)
    high[me] = rounded
    low[me] = (g - rounded.astype(jnp.float32)).astype(jnp.bfloat16)
    images[me, block_rows:, :] = jnp.zeros((8, width), jnp.float32)
    sums[slot] = jnp.zeros((8, width), jnp.float32)
    pl.semaphore_wait(barrier, len(greeted))

    def send(src, dst, which, offset, turn):
        pltpu.make_async_remote_copy(
            src_ref=src, dst_ref=dst, send_sem=send_sem.at[which],
            recv_sem=recv_sem.at[which], device_id=at(offset, turn), device_id_type=MESH,
        ).start()

    def wait(ref, sem):
        pltpu.make_async_copy(ref, ref, sem).wait()

    def gather(vector_of, offsets, group):
        for o in offsets:
            s = lax.rem(me + o, n)
            whole[pl.ds(pl.multiple_of(s * block_rows, block_rows), block_rows), :] = (
                vector_of(s)
            )
        for r in range(block_rows):
            for k in group:
                picked[r : r + 1, k * width : (k + 1) * width] = whole[
                    pl.ds(pattern[k, r], 1), :
                ]

    def multiply(group):
        row = lax.broadcasted_iota(jnp.int32, (ROWS, width), 0)
        out = []
        for base in range(0, block_rows, ROWS):
            left = jnp.concatenate(
                [
                    picked[base : base + ROWS, k * width : (k + 1) * width]
                    for k in group
                ],
                axis=1,
            ).astype(jnp.bfloat16)
            total = jnp.zeros((ROWS, width), jnp.float32)
            for m in range(0, ROWS, 2):
                right = jnp.concatenate(
                    [
                        jnp.concatenate([blocks[base + m + j, k] for k in group], axis=1)
                        for j in range(2)
                    ],
                    axis=0,
                )
                both = lax.dot_general(
                    left, right, (((1,), (1,)), ((), ())),
                    preferred_element_type=jnp.float32,
                )
                total = jnp.where(row == m, both[:, :width], total)
                total = jnp.where(row == m + 1, both[:, width:], total)
            out.append(total)
        return jnp.concatenate(out, axis=0)

    def rowsum(value):
        return jnp.sum(value, axis=0, keepdims=True)

    def total_of(rows):
        return jnp.sum(jnp.sum(rows, axis=0), axis=1, keepdims=True)

    def first(s):
        return high[s].astype(jnp.float32)

    for o in others[::-1]:
        send(high.at[me], high.at[me], 0, o, 0)
    send(high.at[me], high.at[me], 7, half, 0)
    for o in reversed(near):
        send(low.at[me], low.at[me], 1, o, 0)
    fetch.wait()
    load.wait()
    wait(high.at[0], recv_sem.at[7])
    gather(first, [0, half], early)
    part0 = multiply(early)
    wait(high.at[pl.ds(0, len(others))], recv_sem.at[0])
    gather(first, others, late)
    part0 = part0 + multiply(late)

    mine[0] = part0
    send(mine.at[0], theirs.at[0], 2, 0, 1)
    images[me, block_rows : block_rows + 1, :] = rowsum(g * g)
    wait(theirs.at[0], recv_sem.at[2])
    image = part0 + theirs[0]

    images[me, :block_rows, :] = image
    images[me, block_rows + 1 : block_rows + 2, :] = rowsum(g * image)
    tail = pl.ds(block_rows, 4)
    used = pl.ds(0, block_rows + 4)
    for o in reversed(near):
        send(images.at[me, used], images.at[me, used], 3, o, 0)
    for o in far:
        send(images.at[me, tail], images.at[me, tail], 4, o, 0)
    wait(low.at[pl.ds(0, len(near))], recv_sem.at[1])
    wait(images.at[pl.ds(0, len(near)), used], recv_sem.at[3])
    if far:
        wait(images.at[pl.ds(0, len(far)), tail], recv_sem.at[4])
    totals = total_of(images[:, block_rows : block_rows + 4, :])
    norm0 = totals[0:1, :]
    curve0 = totals[1:2, :]
    alpha0 = norm0 / curve0
    r1 = g - alpha0 * image
    gather(
        lambda s: high[s].astype(jnp.float32)
        + (low[s].astype(jnp.float32) - alpha0 * images[s, :block_rows, :]),
        [0] + near,
        range(tiles),
    )
    part1 = multiply(range(tiles))

    sums[slot, 0:1, :] = rowsum(r1 * r1)
    sums[slot, 1:2, :] = rowsum(r1 * part1)
    sums[slot, 2:3, :] = rowsum(r1 * part0 + g * part1)
    for o, c in reversed(peers):
        send(sums.at[slot, pl.ds(0, 4)], sums.at[slot, pl.ds(0, 4)], 5, o, c)
    mine[1] = part1
    send(mine.at[1], theirs.at[1], 6, 0, 1)
    wait(theirs.at[1], recv_sem.at[6])
    image1 = part1 + theirs[1]
    wait(sums.at[pl.ds(0, len(peers)), pl.ds(0, 4)], recv_sem.at[5])
    totals = total_of(sums[...])
    norm1 = totals[0:1, :] * (1.0 / chans)
    beta = norm1 / norm0
    curve1 = totals[1:2, :] + beta * (totals[2:3, :] + beta * curve0)
    alpha1 = norm1 / curve1
    step_out[...] = jnp.broadcast_to(alpha1, (block_rows, width))
    start_out[...] = alpha0 * g
    direction_out[...] = r1 + beta * g
    before_out[...] = r1
    image_out[...] = image1 + beta * image

    wait(high.at[pl.ds(0, len(others))], send_sem.at[0])
    wait(high.at[0], send_sem.at[7])
    wait(low.at[pl.ds(0, len(near))], send_sem.at[1])
    wait(theirs.at[0], send_sem.at[2])
    wait(images.at[pl.ds(0, len(near)), used], send_sem.at[3])
    if far:
        wait(images.at[pl.ds(0, len(far)), tail], send_sem.at[4])
    wait(sums.at[pl.ds(0, len(peers)), pl.ds(0, 4)], send_sem.at[5])
    wait(theirs.at[1], send_sem.at[6])


def solution(mesh):
    n = mesh.shape["stn"]
    chans = mesh.shape["chan"]

    def local(gradient, normal_blocks, pattern):
        _, block_rows, tiles, width, _ = normal_blocks.shape
        f32, bf16 = jnp.float32, jnp.bfloat16
        vector = pltpu.VMEM((block_rows, width), f32)
        vmem = pl.BlockSpec(memory_space=pltpu.VMEM)
        start, alpha, direction, before, image = pl.pallas_call(
            functools.partial(kernel, n, chans),
            out_shape=(vector,) * 5,
            in_specs=[pl.BlockSpec(memory_space=pl.ANY)] * 3,
            out_specs=(vmem,) * 5,
            scratch_shapes=[
                pltpu.SMEM((tiles, block_rows), jnp.int32),
                pltpu.VMEM((block_rows, width), f32),
                pltpu.VMEM((block_rows, tiles, width, width), bf16),
                pltpu.VMEM((n, block_rows, width), bf16),
                pltpu.VMEM((n, block_rows, width), bf16),
                pltpu.VMEM((n, block_rows + 8, width), f32),
                pltpu.VMEM((n * block_rows, width), f32),
                pltpu.VMEM((block_rows, tiles * width), f32),
                pltpu.VMEM((2, block_rows, width), f32),
                pltpu.VMEM((2, block_rows, width), f32),
                pltpu.VMEM((n * chans, 8, width), f32),
                pltpu.SemaphoreType.DMA((3,)),
                pltpu.SemaphoreType.DMA((8,)),
                pltpu.SemaphoreType.DMA((8,)),
            ],
            compiler_params=pltpu.CompilerParams(
                collective_id=0,
                has_side_effects=True,
                vmem_limit_bytes=60 * 1024 * 1024,
            ),
        )(pattern.T, gradient.reshape(block_rows, width), normal_blocks)
        solution = start + alpha * direction
        residual = before - alpha * image
        return solution.reshape(-1), residual.reshape(-1)

    placed = (
        P(("group", "stn")),
        P("chan", ("group", "stn"), None, None, None),
        P(("group", "stn"), None),
    )
    return jax.shard_map(
        local,
        mesh=mesh,
        in_specs=placed,
        out_specs=(P(("group", "stn")), P(("group", "stn"))),
        check_vma=False,
    )
```
